128 devices in a mesh: tm: 4 (over z), chan: 32 (over y, x, core).
Axes of the slice: x: 4, y: 4, z: 4, core: 2. Of those that a mesh axis runs over, the one named last changes fastest.
Arguments:
- records: bfloat16 [16384, 8192], P(('tm', 'chan')), may hold values from -600 to 600
- segment_keep: int32 [16, 256], P('tm', 'chan'), may hold values 0 or 1
Outputs:
- cross: bfloat16 [2, 96, 17, 32, 8192], P(None, 'tm', None, None, 'chan')
The draws below stay inside these ranges and needn't reach their ends.
All inputs are finite; a program needn't handle non-finite values. No bound on the sum of `segment_keep` on one device may be relied on, other than what follows from the above.
Results may differ from the reference program's by a relative error of at most 0.007.
Values may be sent and summed in bfloat16 or wider, within the bound.
A program may use at most 320 MiB of HBM per device.

```python
import math
import jax
import jax.numpy as jnp
from jax import lax

L = 1024
FLO = 10
F = 96
BLK = 32
REACH = 8
SEG = 16
NCH = 8192
NB = 256
NOFF = 17


def draw_records(key, part):
    key = jax.random.fold_in(key, 11)
    key_chan, key_env, key_noise = jax.random.split(key, 3)
    chan_scale = jnp.exp(jax.random.uniform(key_chan, (NCH,), jnp.float32, 0.0, math.log(10.0)))
    envelope = jnp.exp(jax.random.uniform(key_env, (SEG * L // 32,), jnp.float32, 0.0, math.log(10.0)))
    envelope = jnp.repeat(envelope, 32)
    noise = jnp.clip(jax.random.normal(key_noise, (SEG * L, NCH), jnp.float32), -6.0, 6.0)
    return (noise * envelope[:, None] * chan_scale[None, :]).astype(jnp.bfloat16)


def touch_ends(entries, rng, smallest, top_value):
    place = [jax.random.randint(jax.random.fold_in(rng, axis), (), 0, length) for axis, length in enumerate(entries.shape)]
    widest = entries.shape.index(max(entries.shape))
    neighbour = place[:widest] + [(place[widest] + 1) % entries.shape[widest]] + place[widest + 1:]
    return entries.at[tuple(place)].set(smallest).at[tuple(neighbour)].set(top_value)


def setup_inputs(seed: int = 0) -> dict:
    keys = jax.random.split(jax.random.key(seed), 3)
    return {
        "records": draw_records(jax.random.fold_in(keys[2], 71), 0),
        "segment_keep": touch_ends((jax.random.randint(keys[1], (SEG, NB), 0, 4) < 3).astype(jnp.int32), jax.random.fold_in(keys[1], 1), 0, 1),
    }


def taper_table():
    sample_index = jnp.arange(L, dtype=jnp.int32)
    bin_index = FLO + jnp.arange(F, dtype=jnp.int32)
    fraction = (bin_index[:, None] * sample_index[None, :] % L).astype(jnp.float32) / L
    phases = 2.0 * math.pi * fraction
    hann_taper = 0.5 - 0.5 * jnp.cos(2.0 * math.pi * sample_index.astype(jnp.float32) / L)
    weighting = hann_taper / math.sqrt(3.0 * L / 8.0)
    rows_cos = jnp.cos(phases) * weighting[None, :]
    rows_sin = -jnp.sin(phases) * weighting[None, :]
    return jnp.concatenate([rows_cos, rows_sin], 0).astype(jnp.bfloat16)

def reference(records, segment_keep):
    table = taper_table()
    segments_in = records.reshape(SEG, L, NCH)

    def spectrum(segment):
        widened = segment.astype(jnp.float32)
        energy = lax.optimization_barrier(jnp.mean(widened * widened, axis=0))
        raw = jnp.dot(table, segment, preferred_element_type=jnp.float32)
        return raw * lax.rsqrt(energy + 1e-06)[None, :]
    spectra_raw = lax.map(spectrum, segments_in)
    keep_cols = jnp.repeat(segment_keep, BLK, axis=1).astype(jnp.float32)
    spectra = (spectra_raw * keep_cols[:, None, :]).astype(jnp.bfloat16).reshape(SEG, 2, F, NCH)
    pad_width = REACH * BLK
    padded = jnp.pad(spectra, ((0, 0), (0, 0), (0, 0), (pad_width, pad_width)))
    own_blocks = spectra.reshape(SEG, 2, F, NB, BLK).astype(jnp.float32)

    def offset(k):
        partner = lax.dynamic_slice_in_dim(padded, k * BLK, NCH, 3)
        partner = partner.reshape(SEG, 2, F, NB, BLK).astype(jnp.float32)
        turned = jnp.stack([-partner[:, 1], partner[:, 0]], 1)
        real_part = jnp.einsum('xsfna,xsfnb->fbna', own_blocks, partner)
        imag_part = jnp.einsum('xsfna,xsfnb->fbna', own_blocks, turned)
        both = jnp.stack([real_part, imag_part]) * (1.0 / SEG)
        return both.reshape(2, F, BLK, NCH).astype(jnp.bfloat16)
    stacked = lax.map(offset, jnp.arange(NOFF, dtype=jnp.int32))
    return jnp.transpose(stacked, (1, 2, 0, 3, 4))
```

```python
import functools
import math

import jax
import jax.numpy as jnp
import numpy as np
from jax import lax
from jax.experimental import pallas as pl
from jax.experimental.pallas import tpu as pltpu
from jax.sharding import PartitionSpec as P

MESH = pl.DeviceIdType.MESH

L = 1024
FLO = 10
F = 96
BLK = 32
REACH = 8
NOFF = 2 * REACH + 1
SEG = 16

NZ = 4
NY = 4
NX = 4
NC = 2
FSHARE = F // NZ
FG = 8
GROUPS = FSHARE // FG
PIECE = 2 * FSHARE
CH = 256
ROWS = 128
HALF = 128

Y_ORDER = (2, 1, 3, 0)
LINE = tuple((dx, dc) for dx in (2, 1, 3, 0) for dc in (0, 1) if (dx, dc) != (0, 0))


def taper_table():
    t = np.arange(L, dtype=np.int64)
    k = FLO + np.arange(F, dtype=np.int64)
    phase = 2.0 * math.pi * ((k[:, None] * t[None, :]) % L) / L
    taper = (0.5 - 0.5 * np.cos(2.0 * math.pi * t / L)) / math.sqrt(3.0 * L / 8.0)
    both = np.stack([np.cos(phase) * taper, -np.sin(phase) * taper])
    both = both.reshape(2, NZ, GROUPS, FG, L).transpose(1, 2, 0, 3, 4)
    return both.reshape(2 * F, L).astype(np.float32).astype(jnp.bfloat16)


def chan_of(y, x, c):
    return (y * NX + x) * NC + c


def spectra_kernel(
    rec, keep, table, own, left, right,
    land, spec, kown, kbuf,
    a_send, a_recv, a_local, b_send, b_recv, b_local, c_send, c_recv, k_send, k_recv,
):
    z = lax.axis_index("tm")
    ch = lax.axis_index("chan")
    y = ch // (NX * NC)
    x = lax.rem(ch // NC, NX)
    c = lax.rem(ch, NC)
    nchan = NY * NX * NC
    after = lax.rem(ch + 1, nchan)
    before = lax.rem(ch + nchan - 1, nchan)

    def line_peer(dx, dc):
        return lax.rem(x + dx, NX), lax.rem(c + dc, NC)

    barrier = pltpu.get_barrier_semaphore()
    signals = 0
    for dx, dc in LINE:
        px, pc = line_peer(dx, dc)
        pl.semaphore_signal(barrier, inc=1, device_id=(z, chan_of(y, px, pc)), device_id_type=MESH)
        signals += 1
    for dy in range(NY):
        for dz in range(NZ):
            if dy or dz:
                pl.semaphore_signal(
                    barrier, inc=1,
                    device_id=(lax.rem(z + dz, NZ), chan_of(lax.rem(y + dy, NY), x, c)),
                    device_id_type=MESH,
                )
                signals += 1
    for neighbour in (after, before):
        pl.semaphore_signal(barrier, inc=1, device_id=(z, neighbour), device_id_type=MESH)
        signals += 1

    lane_block = lax.broadcasted_iota(jnp.int32, (NZ, CH), 1) // BLK
    spread = jnp.zeros((NZ, CH), jnp.float32)
    for b in range(CH // BLK):
        spread = jnp.where(lane_block == b, keep[:, b : b + 1].astype(jnp.float32), spread)
    kown[0:NY, :] = spread
    kown[NY:8, :] = jnp.zeros((8 - NY, CH), jnp.float32)
    pl.semaphore_wait(barrier, signals)

    mine = pl.multiple_of((x * NC + c) * ROWS, ROWS)
    gathers = []
    for j, dy in enumerate(Y_ORDER):
        q = lax.rem(y + dy, NY)
        stage = []
        for n, (dx, dc) in enumerate(LINE):
            px, pc = line_peer(dx, dc)
            target = chan_of(q, px, pc)
            copy = pltpu.make_async_remote_copy(
                src_ref=rec.at[:, pl.ds(pl.multiple_of(target * CH, CH), CH)],
                dst_ref=land.at[j, pl.ds(mine, ROWS), :],
                send_sem=a_send.at[j, n],
                recv_sem=a_recv.at[j, n],
                device_id=(z, chan_of(y, px, pc)),
                device_id_type=MESH,
            )
            copy.start()
            stage.append(copy)
        local = pltpu.make_async_copy(
            rec.at[:, pl.ds(pl.multiple_of(chan_of(q, x, c) * CH, CH), CH)],
            land.at[j, pl.ds(mine, ROWS), :],
            a_local.at[j],
        )
        local.start()
        gathers.append((stage, local))
        if j == 0:
            keeps = []
            for n, ky in enumerate((1, 2, 3)):
                copy = pltpu.make_async_remote_copy(
                    src_ref=kown,
                    dst_ref=kbuf.at[y],
                    send_sem=k_send.at[n],
                    recv_sem=k_recv.at[n],
                    device_id=(z, chan_of(lax.rem(y + ky, NY), x, c)),
                    device_id_type=MESH,
                )
                copy.start()
                keeps.append(copy)

    def halo(j):
        source = lax.rem(y + NY - Y_ORDER[j], NY)
        copies = []
        for n, (neighbour, into) in enumerate(((after, left), (before, right))):
            copy = pltpu.make_async_remote_copy(
                src_ref=own.at[source],
                dst_ref=into.at[source],
                send_sem=c_send.at[j, n],
                recv_sem=c_recv.at[j, n],
                device_id=(z, neighbour),
                device_id_type=MESH,
            )
            copy.start()
            copies.append(copy)
        return copies

    spreads, halos = [], []
    for j, dy in enumerate(Y_ORDER):
        q = lax.rem(y + dy, NY)
        stage, local = gathers[j]
        for copy in stage:
            copy.wait_recv()
        local.wait()
        if j == 0:
            for copy in keeps:
                copy.wait_recv()
        energy = jnp.zeros((1, CH), jnp.float32)
        for r in range(0, L, ROWS):
            wide = land[j, r : r + ROWS, :].astype(jnp.float32)
            energy = energy + jnp.sum(wide * wide, axis=0, keepdims=True)
        kept = kown[pl.ds(y, 1), :] if dy == 0 else kbuf[q, pl.ds(y, 1), :]
        scale = lax.rsqrt(energy * (1.0 / L) + 1e-06) * kept
        raw = jnp.dot(table[...], land[j], preferred_element_type=jnp.float32)
        spec[j] = (raw * scale).astype(jnp.bfloat16).reshape(NZ, PIECE, CH)
        sent = []
        for dz in (2, 1, 3, 0):
            pz = lax.rem(z + dz, NZ)
            if dy == 0 and dz == 0:
                copy = pltpu.make_async_copy(spec.at[j, pz], own.at[y, z], b_local)
            else:
                copy = pltpu.make_async_remote_copy(
                    src_ref=spec.at[j, pz],
                    dst_ref=own.at[y, z],
                    send_sem=b_send.at[j, dz],
                    recv_sem=b_recv.at[j, dz],
                    device_id=(pz, chan_of(q, x, c)),
                    device_id_type=MESH,
                )
            copy.start()
            sent.append(copy)
        spreads.append(sent)
        if j > 0:
            for copy in spreads[j - 1]:
                copy.wait_recv()
            halos.append(halo(j - 1))
    for copy in spreads[-1][:-1]:
        copy.wait_recv()
    spreads[-1][-1].wait()
    halos.append(halo(NY - 1))

    for stage, _ in gathers:
        for copy in stage:
            copy.wait_send()
    for copy in keeps:
        copy.wait_send()
    for sent in spreads[:-1]:
        for copy in sent:
            copy.wait_send()
    for copy in spreads[-1][:-1]:
        copy.wait_send()
    for pair in halos:
        for copy in pair:
            copy.wait()

    @pl.when(ch == 0)
    def _():
        left[...] = jnp.zeros_like(left)

    @pl.when(ch == nchan - 1)
    def _():
        right[...] = jnp.zeros_like(right)


def gather_spectra(records, keep, table):
    window = jax.ShapeDtypeStruct((NY, NZ, PIECE, CH), jnp.bfloat16)
    vmem = pl.BlockSpec(memory_space=pltpu.VMEM)
    dma = pltpu.SemaphoreType.DMA
    return pl.pallas_call(
        spectra_kernel,
        out_shape=(window, window, window),
        in_specs=[pl.BlockSpec(memory_space=pl.ANY), vmem, vmem],
        out_specs=(vmem, vmem, vmem),
        scratch_shapes=[
            pltpu.VMEM((NY, L, CH), jnp.bfloat16),
            pltpu.VMEM((NY, NZ, PIECE, CH), jnp.bfloat16),
            pltpu.VMEM((8, CH), jnp.float32),
            pltpu.VMEM((NY, 8, CH), jnp.float32),
            dma((NY, len(LINE))), dma((NY, len(LINE))), dma((NY,)),
            dma((NY, NZ)), dma((NY, NZ)), dma,
            dma((NY, 2)), dma((NY, 2)), dma((NY - 1,)), dma((NY - 1,)),
        ],
        compiler_params=pltpu.CompilerParams(
            collective_id=0, has_side_effects=True, vmem_limit_bytes=48 << 20
        ),
        cost_estimate=pl.CostEstimate(
            flops=2 * 2 * F * L * NY * CH, bytes_accessed=2 * NY * L * CH, transcendentals=0
        ),
        name="gather_spectra",
    )(records, keep, table)


def cross_kernel(own, left, right, out, turned, weights):
    f = pl.program_id(0)
    g = f // FG
    f8 = lax.rem(f, FG)
    terms = SEG * 2 * FG

    @pl.when(f8 == 0)
    def _():
        for w, window in enumerate((left, own, right)):
            rows = window[:, :, pl.ds(pl.multiple_of(g * 2 * FG, 2 * FG), 2 * FG), :].reshape(terms, CH)
            turned[w * CH : (w + 1) * CH, :] = rows.T
            if w == 1:
                wide = (rows.astype(jnp.float32) * (1.0 / SEG)).reshape(SEG, 2, FG, CH)
                swapped = jnp.stack([wide[:, 1], -wide[:, 0]], 1)
                plain = wide.reshape(terms, CH).astype(jnp.bfloat16)
                swapped = swapped.reshape(terms, CH).astype(jnp.bfloat16)
                for h in range(2):
                    weights[h, :, 0:HALF] = plain[:, h * HALF : (h + 1) * HALF]
                    weights[h, :, HALF : 2 * HALF] = swapped[:, h * HALF : (h + 1) * HALF]

    row = lax.rem(lax.broadcasted_iota(jnp.int32, (terms, 2 * HALF), 0), FG)
    chosen = jnp.where(row == f8, 1.0, 0.0).astype(jnp.bfloat16)
    lane = lax.broadcasted_iota(jnp.int32, (NOFF * BLK, HALF), 1) // BLK
    rows_needed = NOFF * BLK + HALF - BLK
    for h in range(2):
        product = jnp.dot(
            turned[h * HALF : h * HALF + rows_needed, :],
            weights[h] * chosen,
            preferred_element_type=jnp.float32,
        ).astype(jnp.bfloat16)
        for part in range(2):
            side = product[:, part * HALF : (part + 1) * HALF]
            picked = side[0 : NOFF * BLK]
            for i in range(1, HALF // BLK):
                picked = jnp.where(lane == i, side[i * BLK : i * BLK + NOFF * BLK], picked)
            out[part, 0, :, :, h * HALF : (h + 1) * HALF] = picked.reshape(NOFF, BLK, HALF)


def cross_products(own, left, right):
    terms = SEG * 2 * FG
    vmem = pl.BlockSpec(memory_space=pltpu.VMEM)
    return pl.pallas_call(
        cross_kernel,
        grid=(FSHARE,),
        out_shape=jax.ShapeDtypeStruct((2, FSHARE, NOFF, BLK, CH), jnp.bfloat16),
        in_specs=[vmem, vmem, vmem],
        out_specs=pl.BlockSpec((2, 1, NOFF, BLK, CH), lambda f: (0, f, 0, 0, 0)),
        scratch_shapes=[
            pltpu.VMEM((3 * CH, terms), jnp.bfloat16),
            pltpu.VMEM((2, terms, 2 * HALF), jnp.bfloat16),
        ],
        compiler_params=pltpu.CompilerParams(vmem_limit_bytes=48 << 20),
        name="cross_products",
    )(own, left, right)


def shards(table, records, segment_keep):
    own, left, right = gather_spectra(records, segment_keep, table)
    return cross_products(own, left, right)


def solution(mesh):
    in_specs = (P(None, None), P(("tm", "chan"), None), P("tm", "chan"))
    out_specs = P(None, "tm", None, None, "chan")
    call = jax.shard_map(
        shards, mesh=mesh, in_specs=in_specs, out_specs=out_specs, check_vma=False
    )
    table = taper_table()

    def run(records, segment_keep):
        return call(jnp.asarray(table), records, segment_keep)

    return run
```

```python
import functools
import math

import jax
import jax.numpy as jnp
import numpy as np
from jax import lax
from jax.experimental import pallas as pl
from jax.experimental.pallas import tpu as pltpu
from jax.sharding import PartitionSpec as P

MESH = pl.DeviceIdType.MESH

L = 1024
FLO = 10
F = 96
BLK = 32
REACH = 8
NOFF = 2 * REACH + 1
SEG = 16

NZ = 4
NY = 4
NX = 4
NC = 2
FSHARE = F // NZ
FG = 8
GROUPS = FSHARE // FG
PIECE = 2 * FSHARE
CH = 256
ROWS = 128
HALF = 128

Y_ORDER = (2, 1, 3, 0)
LINE = tuple((dx, dc) for dx in (2, 1, 3, 0) for dc in (0, 1) if (dx, dc) != (0, 0))


def taper_table():
    t = np.arange(L, dtype=np.int64)
    k = FLO + np.arange(F, dtype=np.int64)
    phase = 2.0 * math.pi * ((k[:, None] * t[None, :]) % L) / L
    taper = (0.5 - 0.5 * np.cos(2.0 * math.pi * t / L)) / math.sqrt(3.0 * L / 8.0)
    both = np.stack([np.cos(phase) * taper, -np.sin(phase) * taper])
    both = both.reshape(2, NZ, GROUPS, FG, L).transpose(1, 2, 0, 3, 4)
    return both.reshape(2 * F, L).astype(np.float32).astype(jnp.bfloat16)


def chan_of(y, x, c):
    return (y * NX + x) * NC + c


def spectra_kernel(
    rec, keep, table_hbm, own, left, right,
    land, spec, table, kown, kbuf,
    load, a_send, a_recv, a_local, b_send, b_recv, b_local, c_send, c_recv, k_send, k_recv,
):
    z = lax.axis_index("tm")
    ch = lax.axis_index("chan")
    y = ch // (NX * NC)
    x = lax.rem(ch // NC, NX)
    c = lax.rem(ch, NC)
    nchan = NY * NX * NC
    after = lax.rem(ch + 1, nchan)
    before = lax.rem(ch + nchan - 1, nchan)

    def line_peer(dx, dc):
        return lax.rem(x + dx, NX), lax.rem(c + dc, NC)

    load_table = pltpu.make_async_copy(table_hbm, table, load)
    load_table.start()

    barrier = pltpu.get_barrier_semaphore()
    signals = 0
    for dx, dc in LINE:
        px, pc = line_peer(dx, dc)
        pl.semaphore_signal(barrier, inc=1, device_id=(z, chan_of(y, px, pc)), device_id_type=MESH)
        signals += 1
    for dy in range(NY):
        for dz in range(NZ):
            if dy or dz:
                pl.semaphore_signal(
                    barrier, inc=1,
                    device_id=(lax.rem(z + dz, NZ), chan_of(lax.rem(y + dy, NY), x, c)),
                    device_id_type=MESH,
                )
                signals += 1
    for neighbour in (after, before):
        pl.semaphore_signal(barrier, inc=1, device_id=(z, neighbour), device_id_type=MESH)
        signals += 1

    lane_block = lax.broadcasted_iota(jnp.int32, (1, CH), 1) // BLK
    for s in range(NZ):
        spread = jnp.zeros((1, CH), jnp.int32)
        for b in range(CH // BLK):
            spread = jnp.where(lane_block == b, keep[s, b], spread)
        kown[s : s + 1, :] = spread.astype(jnp.float32)
    kown[NY:8, :] = jnp.zeros((8 - NY, CH), jnp.float32)
    pl.semaphore_wait(barrier, signals)

    mine = pl.multiple_of((x * NC + c) * ROWS, ROWS)
    gathers = []
    for j, dy in enumerate(Y_ORDER):
        q = lax.rem(y + dy, NY)
        stage = []
        for n, (dx, dc) in enumerate(LINE):
            px, pc = line_peer(dx, dc)
            target = chan_of(q, px, pc)
            copy = pltpu.make_async_remote_copy(
                src_ref=rec.at[:, pl.ds(pl.multiple_of(target * CH, CH), CH)],
                dst_ref=land.at[j, pl.ds(mine, ROWS), :],
                send_sem=a_send.at[j, n],
                recv_sem=a_recv.at[j, n],
                device_id=(z, chan_of(y, px, pc)),
                device_id_type=MESH,
            )
            copy.start()
            stage.append(copy)
        local = pltpu.make_async_copy(
            rec.at[:, pl.ds(pl.multiple_of(chan_of(q, x, c) * CH, CH), CH)],
            land.at[j, pl.ds(mine, ROWS), :],
            a_local.at[j],
        )
        local.start()
        gathers.append((stage, local))
        if j == 0:
            keeps = []
            for n, ky in enumerate((1, 2, 3)):
                copy = pltpu.make_async_remote_copy(
                    src_ref=kown,
                    dst_ref=kbuf.at[y],
                    send_sem=k_send.at[n],
                    recv_sem=k_recv.at[n],
                    device_id=(z, chan_of(lax.rem(y + ky, NY), x, c)),
                    device_id_type=MESH,
                )
                copy.start()
                keeps.append(copy)

    def halo(j):
        source = lax.rem(y + NY - Y_ORDER[j], NY)
        copies = []
        for n, (neighbour, into) in enumerate(((after, left), (before, right))):
            copy = pltpu.make_async_remote_copy(
                src_ref=own.at[source],
                dst_ref=into.at[source],
                send_sem=c_send.at[j, n],
                recv_sem=c_recv.at[j, n],
                device_id=(z, neighbour),
                device_id_type=MESH,
            )
            copy.start()
            copies.append(copy)
        return copies

    def sum_squares(j, px, pc):
        rows = pl.ds(pl.multiple_of((px * NC + pc) * ROWS, ROWS), ROWS)
        wide = land[j, rows, :].astype(jnp.float32)
        return jnp.sum(wide * wide, axis=0, keepdims=True)

    spreads, halos = [], []
    for j, dy in enumerate(Y_ORDER):
        q = lax.rem(y + dy, NY)
        stage, local = gathers[j]
        local.wait()
        energy = sum_squares(j, x, c)
        for n, (dx, dc) in enumerate(LINE):
            stage[n].wait_recv()
            energy = energy + sum_squares(j, lax.rem(x + NX - dx, NX), lax.rem(c + dc, NC))
        if j == 0:
            load_table.wait()
            for copy in keeps:
                copy.wait_recv()
        if j == NY - 1:
            for i in range(j):
                for copy in spreads[i]:
                    copy.wait_recv()
                halos.append(halo(i))
        kept = kown[pl.ds(y, 1), :] if dy == 0 else kbuf[q, pl.ds(y, 1), :]
        scale = lax.rsqrt(energy * (1.0 / L) + 1e-06) * kept
        raw = jnp.dot(table[...], land[j], preferred_element_type=jnp.float32)
        spec[j] = (raw * scale).astype(jnp.bfloat16).reshape(NZ, PIECE, CH)
        sent = []
        for dz in (2, 1, 3, 0):
            pz = lax.rem(z + dz, NZ)
            if dy == 0 and dz == 0:
                copy = pltpu.make_async_copy(spec.at[j, pz], own.at[y, z], b_local)
            else:
                copy = pltpu.make_async_remote_copy(
                    src_ref=spec.at[j, pz],
                    dst_ref=own.at[y, z],
                    send_sem=b_send.at[j, dz],
                    recv_sem=b_recv.at[j, dz],
                    device_id=(pz, chan_of(q, x, c)),
                    device_id_type=MESH,
                )
            copy.start()
            sent.append(copy)
        spreads.append(sent)
    for copy in spreads[-1][:-1]:
        copy.wait_recv()
    spreads[-1][-1].wait()
    halos.append(halo(NY - 1))

    for stage, _ in gathers:
        for copy in stage:
            copy.wait_send()
    for copy in keeps:
        copy.wait_send()
    for sent in spreads[:-1]:
        for copy in sent:
            copy.wait_send()
    for copy in spreads[-1][:-1]:
        copy.wait_send()
    for pair in halos:
        for copy in pair:
            copy.wait()

    @pl.when(ch == 0)
    def _():
        left[...] = jnp.zeros_like(left)

    @pl.when(ch == nchan - 1)
    def _():
        right[...] = jnp.zeros_like(right)


def gather_spectra(records, keep, table):
    window = jax.ShapeDtypeStruct((NY, NZ, PIECE, CH), jnp.bfloat16)
    vmem = pl.BlockSpec(memory_space=pltpu.VMEM)
    hbm = pl.BlockSpec(memory_space=pl.ANY)
    dma = pltpu.SemaphoreType.DMA
    return pl.pallas_call(
        spectra_kernel,
        out_shape=(window, window, window),
        in_specs=[hbm, pl.BlockSpec(memory_space=pltpu.SMEM), hbm],
        out_specs=(vmem, vmem, vmem),
        scratch_shapes=[
            pltpu.VMEM((NY, L, CH), jnp.bfloat16),
            pltpu.VMEM((NY, NZ, PIECE, CH), jnp.bfloat16),
            pltpu.VMEM((2 * F, L), jnp.bfloat16),
            pltpu.VMEM((8, CH), jnp.float32),
            pltpu.VMEM((NY, 8, CH), jnp.float32),
            dma, dma((NY, len(LINE))), dma((NY, len(LINE))), dma((NY,)),
            dma((NY, NZ)), dma((NY, NZ)), dma,
            dma((NY, 2)), dma((NY, 2)), dma((NY - 1,)), dma((NY - 1,)),
        ],
        compiler_params=pltpu.CompilerParams(
            collective_id=0, has_side_effects=True, vmem_limit_bytes=211 << 18
        ),
        cost_estimate=pl.CostEstimate(
            flops=2 * 2 * F * L * NY * CH, bytes_accessed=2 * NY * L * CH, transcendentals=0
        ),
        name="gather_spectra",
    )(records, keep, table)


def cross_kernel(own, left, right, out, turned, weights, made, sem):
    terms = SEG * 2 * FG
    reach = NOFF * BLK + HALF - BLK
    lane_block = lax.broadcasted_iota(jnp.int32, (BLK, HALF), 1) // BLK
    row = lax.rem(lax.broadcasted_iota(jnp.int32, (terms, HALF), 0), FG)

    def group(g, carry):
        for w, window in enumerate((left, own, right)):
            rows = window[:, :, pl.ds(pl.multiple_of(g * 2 * FG, 2 * FG), 2 * FG), :].reshape(terms, CH)
            turned[w * CH : (w + 1) * CH, :] = rows.T
            if w == 1:
                wide = (rows.astype(jnp.float32) * (1.0 / SEG)).reshape(SEG, 2, FG, CH)
                plain = wide.reshape(terms, CH).astype(jnp.bfloat16)
                swapped = jnp.stack([wide[:, 1], -wide[:, 0]], 1)
                swapped = swapped.reshape(terms, CH).astype(jnp.bfloat16)
                for h in range(2):
                    weights[h, :, 0:HALF] = plain[:, h * HALF : (h + 1) * HALF]
                    weights[h, :, HALF : 2 * HALF] = swapped[:, h * HALF : (h + 1) * HALF]
        for f8 in range(FG):
            f = g * FG + f8
            chosen = jnp.where(row == f8, 1.0, 0.0).astype(jnp.bfloat16)
            chosen = jnp.concatenate([chosen, chosen], 1)
            for h in range(2):
                product = jnp.dot(
                    turned[h * HALF : h * HALF + reach, :],
                    weights[h] * chosen,
                    preferred_element_type=jnp.float32,
                )
                for part in range(2):
                    side = product[:, part * HALF : (part + 1) * HALF]
                    blocks = [side[r : r + BLK] for r in range(0, reach, BLK)]
                    for k in range(NOFF):
                        picked = blocks[k]
                        for i in range(1, HALF // BLK):
                            picked = jnp.where(lane_block == i, blocks[k + i], picked)
                        made[part, f, k, :, h * HALF : (h + 1) * HALF] = picked.astype(jnp.bfloat16)
            pltpu.make_async_copy(made.at[:, pl.ds(f, 1)], out.at[:, pl.ds(f, 1)], sem).start()
        return carry

    lax.fori_loop(0, GROUPS, group, 0)
    pltpu.make_async_copy(made, out, sem).wait()


def cross_products(own, left, right):
    terms = SEG * 2 * FG
    vmem = pl.BlockSpec(memory_space=pltpu.VMEM)
    result = (2, FSHARE, NOFF, BLK, CH)
    return pl.pallas_call(
        cross_kernel,
        out_shape=jax.ShapeDtypeStruct(result, jnp.bfloat16),
        in_specs=[vmem, vmem, vmem],
        out_specs=pl.BlockSpec(memory_space=pl.ANY),
        scratch_shapes=[
            pltpu.VMEM((3 * CH, terms), jnp.bfloat16),
            pltpu.VMEM((2, terms, 2 * HALF), jnp.bfloat16),
            pltpu.VMEM(result, jnp.bfloat16),
            pltpu.SemaphoreType.DMA,
        ],
        compiler_params=pltpu.CompilerParams(vmem_limit_bytes=48 << 20),
        name="cross_products",
    )(own, left, right)


def shards(table, records, segment_keep):
    own, left, right = gather_spectra(records, segment_keep, table)
    return cross_products(own, left, right)


def solution(mesh):
    in_specs = (P(None, None), P(("tm", "chan"), None), P("tm", "chan"))
    out_specs = P(None, "tm", None, None, "chan")
    call = jax.shard_map(
        shards, mesh=mesh, in_specs=in_specs, out_specs=out_specs, check_vma=False
    )
    table = taper_table()

    def run(records, segment_keep):
        return call(jnp.asarray(table), records, segment_keep)

    return run
```

```python
import functools
import math

import jax
import jax.numpy as jnp
import numpy as np
from jax import lax
from jax.experimental import pallas as pl
from jax.experimental.pallas import tpu as pltpu
from jax.sharding import PartitionSpec as P

MESH = pl.DeviceIdType.MESH

L = 1024
FLO = 10
F = 96
BLK = 32
REACH = 8
NOFF = 2 * REACH + 1
SEG = 16

NZ = 4
NY = 4
NX = 4
NC = 2
FSHARE = F // NZ
FG = 8
GROUPS = FSHARE // FG
PIECE = 2 * FSHARE
CH = 256
ROWS = 128
HALF = 128

STAGES = ((2, 0, 256), (1, 0, 256), (3, 0, 256), (0, 0, 256))
NS = len(STAGES)
AHEAD = 2
LAG = 1

LINE = tuple((dx, dc) for dx in (1, 3, 0) for dc in (0, 1) if (dx, dc) != (0, 0))


def taper_table():
    t = np.arange(L, dtype=np.int64)
    k = FLO + np.arange(F, dtype=np.int64)
    phase = 2.0 * math.pi * ((k[:, None] * t[None, :]) % L) / L
    taper = (0.5 - 0.5 * np.cos(2.0 * math.pi * t / L)) / math.sqrt(3.0 * L / 8.0)
    both = np.stack([np.cos(phase) * taper, -np.sin(phase) * taper])
    both = both.reshape(2, NZ, GROUPS, FG, L).transpose(1, 2, 0, 3, 4)
    return both.reshape(2 * F, L).astype(np.float32).astype(jnp.bfloat16)


def chan_of(y, x, c):
    return (y * NX + x) * NC + c


def spectra_kernel(
    rec, keep, table_hbm, own, left, right,
    near, helped, partial, summed, spec, table, kown, kbuf,
    load, a_send, a_recv, a_local, p_send, p_recv,
    b_send, b_recv, b_local, c_send, c_recv, k_send, k_recv,
):
    z = lax.axis_index("tm")
    ch = lax.axis_index("chan")
    y = ch // (NX * NC)
    x = lax.rem(ch // NC, NX)
    c = lax.rem(ch, NC)
    nchan = NY * NX * NC
    after = lax.rem(ch + 1, nchan)
    before = lax.rem(ch + nchan - 1, nchan)

    def side(core):
        return 1 - 2 * core

    def along(steps):
        return lax.rem(x + NX + steps, NX)

    ahead, behind = along(side(c)), along(-side(c))

    load_table = pltpu.make_async_copy(table_hbm, table, load)
    load_table.start()

    barrier = pltpu.get_barrier_semaphore()
    signals = 0
    for dx, dc in LINE:
        peer = chan_of(y, lax.rem(x + dx, NX), lax.rem(c + dc, NC))
        pl.semaphore_signal(barrier, inc=1, device_id=(z, peer), device_id_type=MESH)
        signals += 1
    for dy in range(NY):
        for dz in range(NZ):
            if dy or dz:
                pl.semaphore_signal(
                    barrier, inc=1,
                    device_id=(lax.rem(z + dz, NZ), chan_of(lax.rem(y + dy, NY), x, c)),
                    device_id_type=MESH,
                )
                signals += 1
    for neighbour in (after, before):
        pl.semaphore_signal(barrier, inc=1, device_id=(z, neighbour), device_id_type=MESH)
        signals += 1

    pl.semaphore_wait(barrier, signals)

    def rows_of(group_x, group_c, j):
        dy, first, width = STAGES[j]
        column = chan_of(lax.rem(y + dy, NY), group_x, group_c) * CH + first
        return rec.at[:, pl.ds(pl.multiple_of(column, HALF), width)]

    def place(buffer, j, part):
        rows = pl.ds(pl.multiple_of(part * NC * ROWS + c * ROWS, ROWS), ROWS)
        return buffer.at[j, rows, pl.ds(0, STAGES[j][2])]

    def gather(j):
        to_helped, to_near = [], []
        n = 0
        for e in (0, 1):
            core = lax.rem(c + e, NC)
            s = side(core)
            for copies, buffer, part, group_x, target_x in (
                (to_helped, helped, 1, along(2), along(-s)),
                (to_near, near, 1, along(s), along(s)),
                (to_helped, helped, 0, along(-s), x),
                (to_near, near, 0, x, x),
            ):
                source, target = rows_of(group_x, core, j), place(buffer, j, part)
                if part == 0 and e == 0:
                    copy = pltpu.make_async_copy(
                        source, target, a_local.at[j, 0 if buffer is helped else 1]
                    )
                else:
                    copy = pltpu.make_async_remote_copy(
                        src_ref=source,
                        dst_ref=target,
                        send_sem=a_send.at[j, n],
                        recv_sem=a_recv.at[j, n],
                        device_id=(z, chan_of(y, target_x, core)),
                        device_id_type=MESH,
                    )
                    n += 1
                copy.start()
                copies.append((copy, part == 0 and e == 0))
        return to_helped, to_near

    gathers = [gather(j) for j in range(AHEAD)]
    lane_block = lax.broadcasted_iota(jnp.int32, (1, CH), 1) // BLK
    for s in range(NZ):
        spread = jnp.zeros((1, CH), jnp.int32)
        for b in range(CH // BLK):
            spread = jnp.where(lane_block == b, keep[s, b], spread)
        kown[s : s + 1, :] = spread.astype(jnp.float32)
    kown[NY:8, :] = jnp.zeros((8 - NY, CH), jnp.float32)
    keeps = []
    for n, ky in enumerate((1, 2, 3)):
        copy = pltpu.make_async_remote_copy(
            src_ref=kown,
            dst_ref=kbuf.at[y],
            send_sem=k_send.at[n],
            recv_sem=k_recv.at[n],
            device_id=(z, chan_of(lax.rem(y + ky, NY), x, c)),
            device_id_type=MESH,
        )
        copy.start()
        keeps.append(copy)

    def half_sum(buffer, j, chips):
        width = STAGES[j][2]
        total = jnp.zeros((2 * F, width), jnp.float32)
        energy = jnp.zeros((1, width), jnp.float32)
        for part, chip in enumerate(chips):
            data = buffer[j, part * NC * ROWS : (part + 1) * NC * ROWS, 0:width]
            columns = pl.ds(pl.multiple_of(chip * (NC * ROWS), NC * ROWS), NC * ROWS)
            total = total + jnp.dot(table[:, columns], data, preferred_element_type=jnp.float32)
            wide = data.astype(jnp.float32)
            energy = energy + jnp.sum(wide * wide, axis=0, keepdims=True)
        return total, energy

    def arrive(copies):
        for copy, local in copies:
            copy.wait() if local else copy.wait_recv()

    def pass_on(j):
        arrive(gathers[j][0])
        if len(gathers) < NS:
            gathers.append(gather(len(gathers)))
        total, energy = half_sum(helped, j, (x, ahead))
        width = STAGES[j][2]
        partial[j, 0 : 2 * F, 0:width] = total
        partial[j, 2 * F :, 0:width] = jnp.broadcast_to(energy, (8, width))
        copy = pltpu.make_async_remote_copy(
            src_ref=partial.at[j, :, pl.ds(0, width)],
            dst_ref=summed.at[j, :, pl.ds(0, width)],
            send_sem=p_send.at[j],
            recv_sem=p_recv.at[j],
            device_id=(z, chan_of(y, behind, c)),
            device_id_type=MESH,
        )
        copy.start()
        passed.append(copy)

    def halo(j):
        dy, first, width = STAGES[j]
        source = lax.rem(y + NY - dy, NY)
        copies = []
        for n, (neighbour, into) in enumerate(((after, left), (before, right))):
            copy = pltpu.make_async_remote_copy(
                src_ref=own.at[source, :, :, pl.ds(first, width)],
                dst_ref=into.at[source, :, :, pl.ds(first, width)],
                send_sem=c_send.at[j, n],
                recv_sem=c_recv.at[j, n],
                device_id=(z, neighbour),
                device_id_type=MESH,
            )
            copy.start()
            copies.append(copy)
        return copies

    def spread_arrived(j):
        for copy, local in spreads[j]:
            copy.wait() if local else copy.wait_recv()

    def finish(j):
        dy, first, width = STAGES[j]
        q = lax.rem(y + dy, NY)
        arrive(gathers[j][1])
        total, energy = half_sum(near, j, (x, behind))
        passed[j].wait_recv()
        for i in range(len(halos), j - 1):
            spread_arrived(i)
            halos.append(halo(i))
        energy = energy + summed[j, 2 * F : 2 * F + 1, 0:width]
        lanes = slice(first, first + width)
        kept = kown[pl.ds(y, 1), lanes] if dy == 0 else kbuf[q, pl.ds(y, 1), lanes]
        scale = lax.rsqrt(energy * (1.0 / L) + 1e-06) * kept
        raw = total + summed[j, 0 : 2 * F, 0:width]
        spec[j, :, :, 0:width] = (raw * scale).astype(jnp.bfloat16).reshape(NZ, PIECE, width)
        sent = []
        for dz in (2, 1, 3, 0):
            pz = lax.rem(z + dz, NZ)
            source = spec.at[j, pz, :, pl.ds(0, width)]
            target = own.at[y, z, :, pl.ds(first, width)]
            if dy == 0 and dz == 0:
                copy = pltpu.make_async_copy(source, target, b_local.at[j])
            else:
                copy = pltpu.make_async_remote_copy(
                    src_ref=source,
                    dst_ref=target,
                    send_sem=b_send.at[j, dz],
                    recv_sem=b_recv.at[j, dz],
                    device_id=(pz, chan_of(q, x, c)),
                    device_id_type=MESH,
                )
            copy.start()
            sent.append((copy, dy == 0 and dz == 0))
        spreads.append(sent)

    load_table.wait()
    passed, spreads, halos = [], [], []
    for j in range(NS):
        pass_on(j)
        if j == 0:
            for copy in keeps:
                copy.wait_recv()
        if j >= LAG:
            finish(j - LAG)
    for j in range(NS - LAG, NS):
        finish(j)
    for j in range(len(halos), NS):
        spread_arrived(j)
        halos.append(halo(j))

    for stage in gathers:
        for copies in stage:
            for copy, local in copies:
                if not local:
                    copy.wait_send()
    for copy in keeps + passed:
        copy.wait_send()
    for sent in spreads:
        for copy, local in sent:
            if not local:
                copy.wait_send()
    for pair in halos:
        for copy in pair:
            copy.wait()

    @pl.when(ch == 0)
    def _():
        left[...] = jnp.zeros_like(left)

    @pl.when(ch == nchan - 1)
    def _():
        right[...] = jnp.zeros_like(right)


def gather_spectra(records, keep, table):
    window = jax.ShapeDtypeStruct((NY, NZ, PIECE, CH), jnp.bfloat16)
    vmem = pl.BlockSpec(memory_space=pltpu.VMEM)
    hbm = pl.BlockSpec(memory_space=pl.ANY)
    dma = pltpu.SemaphoreType.DMA
    half = pltpu.VMEM((NS, 2 * NC * ROWS, CH), jnp.bfloat16)
    sums = pltpu.VMEM((NS, 2 * F + 8, CH), jnp.float32)
    return pl.pallas_call(
        spectra_kernel,
        out_shape=(window, window, window),
        in_specs=[hbm, pl.BlockSpec(memory_space=pltpu.SMEM), hbm],
        out_specs=(vmem, vmem, vmem),
        scratch_shapes=[
            half, half, sums, sums,
            pltpu.VMEM((NS, NZ, PIECE, CH), jnp.bfloat16),
            pltpu.VMEM((2 * F, L), jnp.bfloat16),
            pltpu.VMEM((8, CH), jnp.float32),
            pltpu.VMEM((NY, 8, CH), jnp.float32),
            dma, dma((NS, 6)), dma((NS, 6)), dma((NS, 2)), dma((NS,)), dma((NS,)),
            dma((NS, NZ)), dma((NS, NZ)), dma((NS,)),
            dma((NS, 2)), dma((NS, 2)), dma((NY - 1,)), dma((NY - 1,)),
        ],
        compiler_params=pltpu.CompilerParams(
            collective_id=0, has_side_effects=True, vmem_limit_bytes=211 << 18
        ),
        cost_estimate=pl.CostEstimate(
            flops=2 * 2 * F * L * NY * CH, bytes_accessed=2 * NY * L * CH, transcendentals=0
        ),
        name="gather_spectra",
    )(records, keep, table)


def cross_kernel(own, left, right, out, turned, weights, made, sem):
    terms = SEG * 2 * FG
    reach = NOFF * BLK + HALF - BLK
    lane_block = lax.broadcasted_iota(jnp.int32, (BLK, HALF), 1) // BLK
    row = lax.rem(lax.broadcasted_iota(jnp.int32, (terms, HALF), 0), FG)

    def group(g, carry):
        for w, window in enumerate((left, own, right)):
            rows = window[:, :, pl.ds(pl.multiple_of(g * 2 * FG, 2 * FG), 2 * FG), :].reshape(terms, CH)
            turned[w * CH : (w + 1) * CH, :] = rows.T
            if w == 1:
                wide = (rows.astype(jnp.float32) * (1.0 / SEG)).reshape(SEG, 2, FG, CH)
                plain = wide.reshape(terms, CH).astype(jnp.bfloat16)
                swapped = jnp.stack([wide[:, 1], -wide[:, 0]], 1)
                swapped = swapped.reshape(terms, CH).astype(jnp.bfloat16)
                for h in range(2):
                    weights[h, :, 0:HALF] = plain[:, h * HALF : (h + 1) * HALF]
                    weights[h, :, HALF : 2 * HALF] = swapped[:, h * HALF : (h + 1) * HALF]
        for f8 in range(FG):
            f = g * FG + f8
            chosen = jnp.where(row == f8, 1.0, 0.0).astype(jnp.bfloat16)
            chosen = jnp.concatenate([chosen, chosen], 1)
            for h in range(2):
                product = jnp.dot(
                    turned[h * HALF : h * HALF + reach, :],
                    weights[h] * chosen,
                    preferred_element_type=jnp.float32,
                )
                for part in range(2):
                    side = product[:, part * HALF : (part + 1) * HALF]
                    blocks = [side[r : r + BLK] for r in range(0, reach, BLK)]
                    for k in range(NOFF):
                        picked = blocks[k]
                        for i in range(1, HALF // BLK):
                            picked = jnp.where(lane_block == i, blocks[k + i], picked)
                        made[part, f, k, :, h * HALF : (h + 1) * HALF] = picked.astype(jnp.bfloat16)
            pltpu.make_async_copy(made.at[:, pl.ds(f, 1)], out.at[:, pl.ds(f, 1)], sem).start()
        return carry

    lax.fori_loop(0, GROUPS, group, 0)
    pltpu.make_async_copy(made, out, sem).wait()


def cross_products(own, left, right):
    terms = SEG * 2 * FG
    vmem = pl.BlockSpec(memory_space=pltpu.VMEM)
    result = (2, FSHARE, NOFF, BLK, CH)
    return pl.pallas_call(
        cross_kernel,
        out_shape=jax.ShapeDtypeStruct(result, jnp.bfloat16),
        in_specs=[vmem, vmem, vmem],
        out_specs=pl.BlockSpec(memory_space=pl.ANY),
        scratch_shapes=[
            pltpu.VMEM((3 * CH, terms), jnp.bfloat16),
            pltpu.VMEM((2, terms, 2 * HALF), jnp.bfloat16),
            pltpu.VMEM(result, jnp.bfloat16),
            pltpu.SemaphoreType.DMA,
        ],
        compiler_params=pltpu.CompilerParams(vmem_limit_bytes=48 << 20),
        name="cross_products",
    )(own, left, right)


def shards(table, records, segment_keep):
    own, left, right = gather_spectra(records, segment_keep, table)
    return cross_products(own, left, right)


def solution(mesh):
    in_specs = (P(None, None), P(("tm", "chan"), None), P("tm", "chan"))
    out_specs = P(None, "tm", None, None, "chan")
    call = jax.shard_map(
        shards, mesh=mesh, in_specs=in_specs, out_specs=out_specs, check_vma=False
    )
    table = taper_table()

    def run(records, segment_keep):
        return call(jnp.asarray(table), records, segment_keep)

    return run
```

```python
import functools
import math

import jax
import jax.numpy as jnp
import numpy as np
from jax import lax
from jax.experimental import pallas as pl
from jax.experimental.pallas import tpu as pltpu
from jax.sharding import PartitionSpec as P

MESH = pl.DeviceIdType.MESH

L = 1024
FLO = 10
F = 96
BLK = 32
REACH = 8
NOFF = 2 * REACH + 1
SEG = 16

NZ = 4
NY = 4
NX = 4
NC = 2
FSHARE = F // NZ
FG = 8
GROUPS = FSHARE // FG
PIECE = 2 * FSHARE
CH = 256
ROWS = 128
HALF = 128

STAGES = ((2, 0, 256), (1, 0, 256), (3, 0, 256), (0, 0, 256))
NS = len(STAGES)
AHEAD = 2
LAG = 1

LINE = tuple((dx, dc) for dx in (1, 3, 0) for dc in (0, 1) if (dx, dc) != (0, 0))


def taper_table():
    t = np.arange(L, dtype=np.int64)
    k = FLO + np.arange(F, dtype=np.int64)
    phase = 2.0 * math.pi * ((k[:, None] * t[None, :]) % L) / L
    taper = (0.5 - 0.5 * np.cos(2.0 * math.pi * t / L)) / math.sqrt(3.0 * L / 8.0)
    both = np.stack([np.cos(phase) * taper, -np.sin(phase) * taper])
    both = both.reshape(2, NZ, GROUPS, FG, L).transpose(1, 2, 0, 3, 4)
    return both.reshape(2 * F, L).astype(np.float32).astype(jnp.bfloat16)


def chan_of(y, x, c):
    return (y * NX + x) * NC + c


def spectra_kernel(
    rec, keep, table_hbm, own, left, right,
    near, helped, partial, summed, spec, table, kown, kbuf,
    load, a_send, a_recv, a_local, p_send, p_recv,
    b_send, b_recv, b_local, c_send, c_recv, k_send, k_recv,
):
    z = lax.axis_index("tm")
    ch = lax.axis_index("chan")
    y = ch // (NX * NC)
    x = lax.rem(ch // NC, NX)
    c = lax.rem(ch, NC)
    nchan = NY * NX * NC
    after = lax.rem(ch + 1, nchan)
    before = lax.rem(ch + nchan - 1, nchan)

    def side(core):
        return 1 - 2 * core

    def along(steps):
        return lax.rem(x + NX + steps, NX)

    ahead, behind = along(side(c)), along(-side(c))

    load_table = pltpu.make_async_copy(table_hbm, table, load)
    load_table.start()

    barrier = pltpu.get_barrier_semaphore()
    signals = 0
    for dx, dc in LINE:
        peer = chan_of(y, lax.rem(x + dx, NX), lax.rem(c + dc, NC))
        pl.semaphore_signal(barrier, inc=1, device_id=(z, peer), device_id_type=MESH)
        signals += 1
    for dy in range(NY):
        for dz in range(NZ):
            if dy or dz:
                pl.semaphore_signal(
                    barrier, inc=1,
                    device_id=(lax.rem(z + dz, NZ), chan_of(lax.rem(y + dy, NY), x, c)),
                    device_id_type=MESH,
                )
                signals += 1
    for neighbour in (after, before):
        pl.semaphore_signal(barrier, inc=1, device_id=(z, neighbour), device_id_type=MESH)
        signals += 1

    pl.semaphore_wait(barrier, signals)

    def rows_of(group_x, group_c, j):
        dy, first, width = STAGES[j]
        column = chan_of(lax.rem(y + dy, NY), group_x, group_c) * CH + first
        return rec.at[:, pl.ds(pl.multiple_of(column, HALF), width)]

    def place(buffer, j, part):
        rows = pl.ds(pl.multiple_of(part * NC * ROWS + c * ROWS, ROWS), ROWS)
        return buffer.at[j, rows, pl.ds(0, STAGES[j][2])]

    def gather(j):
        to_helped, to_near = [], []
        n = 0
        for e in (0, 1):
            core = lax.rem(c + e, NC)
            s = side(core)
            for copies, buffer, part, group_x, target_x in (
                (to_helped, helped, 1, along(2), along(-s)),
                (to_near, near, 1, along(s), along(s)),
                (to_helped, helped, 0, along(-s), x),
                (to_near, near, 0, x, x),
            ):
                source, target = rows_of(group_x, core, j), place(buffer, j, part)
                if part == 0 and e == 0:
                    copy = pltpu.make_async_copy(
                        source, target, a_local.at[j, 0 if buffer is helped else 1]
                    )
                else:
                    copy = pltpu.make_async_remote_copy(
                        src_ref=source,
                        dst_ref=target,
                        send_sem=a_send.at[j, n],
                        recv_sem=a_recv.at[j, n],
                        device_id=(z, chan_of(y, target_x, core)),
                        device_id_type=MESH,
                    )
                    n += 1
                copy.start()
                copies.append((copy, part == 0 and e == 0))
        return to_helped, to_near

    gathers = [gather(j) for j in range(AHEAD)]
    lane_block = lax.broadcasted_iota(jnp.int32, (1, CH), 1) // BLK
    for s in range(NZ):
        spread = jnp.zeros((1, CH), jnp.int32)
        for b in range(CH // BLK):
            spread = jnp.where(lane_block == b, keep[s, b], spread)
        kown[s : s + 1, :] = spread.astype(jnp.float32)
    kown[NY:8, :] = jnp.zeros((8 - NY, CH), jnp.float32)
    keeps = []
    for n, ky in enumerate((1, 2, 3)):
        copy = pltpu.make_async_remote_copy(
            src_ref=kown,
            dst_ref=kbuf.at[y],
            send_sem=k_send.at[n],
            recv_sem=k_recv.at[n],
            device_id=(z, chan_of(lax.rem(y + ky, NY), x, c)),
            device_id_type=MESH,
        )
        copy.start()
        keeps.append(copy)

    def half_sum(buffer, j, chips):
        width = STAGES[j][2]
        total = jnp.zeros((2 * F, width), jnp.float32)
        energy = jnp.zeros((1, width), jnp.float32)
        for part, chip in enumerate(chips):
            data = buffer[j, part * NC * ROWS : (part + 1) * NC * ROWS, 0:width]
            columns = pl.ds(pl.multiple_of(chip * (NC * ROWS), NC * ROWS), NC * ROWS)
            total = total + jnp.dot(table[:, columns], data, preferred_element_type=jnp.float32)
            wide = data.astype(jnp.float32)
            energy = energy + jnp.sum(wide * wide, axis=0, keepdims=True)
        return total, energy

    def arrive(copies):
        for copy, local in copies:
            copy.wait() if local else copy.wait_recv()

    def pass_on(j):
        arrive(gathers[j][0])
        if len(gathers) < NS:
            gathers.append(gather(len(gathers)))
        total, energy = half_sum(helped, j, (x, ahead))
        width = STAGES[j][2]
        partial[j, 0 : 2 * F, 0:width] = total
        partial[j, 2 * F :, 0:width] = jnp.broadcast_to(energy, (8, width))
        copy = pltpu.make_async_remote_copy(
            src_ref=partial.at[j, :, pl.ds(0, width)],
            dst_ref=summed.at[j, :, pl.ds(0, width)],
            send_sem=p_send.at[j],
            recv_sem=p_recv.at[j],
            device_id=(z, chan_of(y, behind, c)),
            device_id_type=MESH,
        )
        copy.start()
        passed.append(copy)

    def halo(j):
        dy, first, width = STAGES[j]
        source = lax.rem(y + NY - dy, NY)
        copies = []
        for n, (neighbour, into) in enumerate(((after, left), (before, right))):
            copy = pltpu.make_async_remote_copy(
                src_ref=own.at[source, :, :, pl.ds(first, width)],
                dst_ref=into.at[source, :, :, pl.ds(first, width)],
                send_sem=c_send.at[j, n],
                recv_sem=c_recv.at[j, n],
                device_id=(z, neighbour),
                device_id_type=MESH,
            )
            copy.start()
            copies.append(copy)
        return copies

    def spread_arrived(j):
        for copy, local in spreads[j]:
            copy.wait() if local else copy.wait_recv()

    def finish(j):
        dy, first, width = STAGES[j]
        q = lax.rem(y + dy, NY)
        arrive(gathers[j][1])
        total, energy = half_sum(near, j, (x, behind))
        passed[j].wait_recv()
        energy = energy + summed[j, 2 * F : 2 * F + 1, 0:width]
        lanes = slice(first, first + width)
        kept = kown[pl.ds(y, 1), lanes] if dy == 0 else kbuf[q, pl.ds(y, 1), lanes]
        scale = lax.rsqrt(energy * (1.0 / L) + 1e-06) * kept
        raw = total + summed[j, 0 : 2 * F, 0:width]
        spec[j, :, :, 0:width] = (raw * scale).astype(jnp.bfloat16).reshape(NZ, PIECE, width)
        sent = []
        for dz in (2, 1, 3, 0):
            pz = lax.rem(z + dz, NZ)
            source = spec.at[j, pz, :, pl.ds(0, width)]
            target = own.at[y, z, :, pl.ds(first, width)]
            if dy == 0 and dz == 0:
                copy = pltpu.make_async_copy(source, target, b_local.at[j])
            else:
                copy = pltpu.make_async_remote_copy(
                    src_ref=source,
                    dst_ref=target,
                    send_sem=b_send.at[j, dz],
                    recv_sem=b_recv.at[j, dz],
                    device_id=(pz, chan_of(q, x, c)),
                    device_id_type=MESH,
                )
            copy.start()
            sent.append((copy, dy == 0 and dz == 0))
        spreads.append(sent)

    load_table.wait()
    passed, spreads, halos = [], [], []
    for j in range(NS):
        pass_on(j)
        for i in range(len(halos), j - 2):
            spread_arrived(i)
            halos.append(halo(i))
        if j == 0:
            for copy in keeps:
                copy.wait_recv()
        if j >= LAG:
            finish(j - LAG)
    for j in range(NS - LAG, NS):
        finish(j)
    for j in range(len(halos), NS):
        spread_arrived(j)
        halos.append(halo(j))

    for stage in gathers:
        for copies in stage:
            for copy, local in copies:
                if not local:
                    copy.wait_send()
    for copy in keeps + passed:
        copy.wait_send()
    for sent in spreads:
        for copy, local in sent:
            if not local:
                copy.wait_send()
    for pair in halos:
        for copy in pair:
            copy.wait()

    @pl.when(ch == 0)
    def _():
        left[...] = jnp.zeros_like(left)

    @pl.when(ch == nchan - 1)
    def _():
        right[...] = jnp.zeros_like(right)


def gather_spectra(records, keep, table):
    window = jax.ShapeDtypeStruct((NY, NZ, PIECE, CH), jnp.bfloat16)
    vmem = pl.BlockSpec(memory_space=pltpu.VMEM)
    hbm = pl.BlockSpec(memory_space=pl.ANY)
    dma = pltpu.SemaphoreType.DMA
    half = pltpu.VMEM((NS, 2 * NC * ROWS, CH), jnp.bfloat16)
    sums = pltpu.VMEM((NS, 2 * F + 8, CH), jnp.float32)
    return pl.pallas_call(
        spectra_kernel,
        out_shape=(window, window, window),
        in_specs=[hbm, pl.BlockSpec(memory_space=pltpu.SMEM), hbm],
        out_specs=(vmem, vmem, vmem),
        scratch_shapes=[
            half, half, sums, sums,
            pltpu.VMEM((NS, NZ, PIECE, CH), jnp.bfloat16),
            pltpu.VMEM((2 * F, L), jnp.bfloat16),
            pltpu.VMEM((8, CH), jnp.float32),
            pltpu.VMEM((NY, 8, CH), jnp.float32),
            dma, dma((NS, 6)), dma((NS, 6)), dma((NS, 2)), dma((NS,)), dma((NS,)),
            dma((NS, NZ)), dma((NS, NZ)), dma((NS,)),
            dma((NS, 2)), dma((NS, 2)), dma((NY - 1,)), dma((NY - 1,)),
        ],
        compiler_params=pltpu.CompilerParams(
            collective_id=0, has_side_effects=True, vmem_limit_bytes=211 << 18
        ),
        cost_estimate=pl.CostEstimate(
            flops=2 * 2 * F * L * NY * CH, bytes_accessed=2 * NY * L * CH, transcendentals=0
        ),
        name="gather_spectra",
    )(records, keep, table)


def cross_kernel(own, left, right, out, turned, weights, made, sem):
    terms = SEG * 2 * FG
    reach = NOFF * BLK + HALF - BLK
    lane_block = lax.broadcasted_iota(jnp.int32, (BLK, HALF), 1) // BLK
    row = lax.rem(lax.broadcasted_iota(jnp.int32, (terms, HALF), 0), FG)

    def prepare(g):
        for w, window in enumerate((left, own, right)):
            rows = window[:, :, g * 2 * FG : (g + 1) * 2 * FG, :].reshape(terms, CH)
            turned[g, w * CH : (w + 1) * CH, :] = rows.T
            if w == 1:
                wide = (rows.astype(jnp.float32) * (1.0 / SEG)).reshape(SEG, 2, FG, CH)
                plain = wide.reshape(terms, CH).astype(jnp.bfloat16)
                swapped = jnp.stack([wide[:, 1], -wide[:, 0]], 1)
                swapped = swapped.reshape(terms, CH).astype(jnp.bfloat16)
                for h in range(2):
                    weights[g, h, :, 0:HALF] = plain[:, h * HALF : (h + 1) * HALF]
                    weights[g, h, :, HALF : 2 * HALF] = swapped[:, h * HALF : (h + 1) * HALF]

    prepare(0)
    for g in range(GROUPS):
        for f8 in range(FG):
            if f8 == FG // 2 and g + 1 < GROUPS:
                prepare(g + 1)
            f = g * FG + f8
            chosen = jnp.where(row == f8, 1.0, 0.0).astype(jnp.bfloat16)
            chosen = jnp.concatenate([chosen, chosen], 1)
            for h in range(2):
                product = jnp.dot(
                    turned[g, h * HALF : h * HALF + reach, :],
                    weights[g, h] * chosen,
                    preferred_element_type=jnp.float32,
                )
                for part in range(2):
                    side = product[:, part * HALF : (part + 1) * HALF]
                    blocks = [side[r : r + BLK] for r in range(0, reach, BLK)]
                    for k in range(NOFF):
                        picked = blocks[k]
                        for i in range(1, HALF // BLK):
                            picked = jnp.where(lane_block == i, blocks[k + i], picked)
                        made[part, f, k, :, h * HALF : (h + 1) * HALF] = picked.astype(jnp.bfloat16)
            pltpu.make_async_copy(made.at[:, pl.ds(f, 1)], out.at[:, pl.ds(f, 1)], sem).start()
    pltpu.make_async_copy(made, out, sem).wait()


def cross_products(own, left, right):
    terms = SEG * 2 * FG
    vmem = pl.BlockSpec(memory_space=pltpu.VMEM)
    result = (2, FSHARE, NOFF, BLK, CH)
    return pl.pallas_call(
        cross_kernel,
        out_shape=jax.ShapeDtypeStruct(result, jnp.bfloat16),
        in_specs=[vmem, vmem, vmem],
        out_specs=pl.BlockSpec(memory_space=pl.ANY),
        scratch_shapes=[
            pltpu.VMEM((GROUPS, 3 * CH, terms), jnp.bfloat16),
            pltpu.VMEM((GROUPS, 2, terms, 2 * HALF), jnp.bfloat16),
            pltpu.VMEM(result, jnp.bfloat16),
            pltpu.SemaphoreType.DMA,
        ],
        compiler_params=pltpu.CompilerParams(vmem_limit_bytes=48 << 20),
        name="cross_products",
    )(own, left, right)


def shards(table, records, segment_keep):
    own, left, right = gather_spectra(records, segment_keep, table)
    return cross_products(own, left, right)


def solution(mesh):
    in_specs = (P(None, None), P(("tm", "chan"), None), P("tm", "chan"))
    out_specs = P(None, "tm", None, None, "chan")
    call = jax.shard_map(
        shards, mesh=mesh, in_specs=in_specs, out_specs=out_specs, check_vma=False
    )
    table = taper_table()

    def run(records, segment_keep):
        return call(jnp.asarray(table), records, segment_keep)

    return run
```

```python
import functools
import math

import jax
import jax.numpy as jnp
import numpy as np
from jax import lax
from jax.experimental import pallas as pl
from jax.experimental.pallas import tpu as pltpu
from jax.sharding import PartitionSpec as P

MESH = pl.DeviceIdType.MESH

L = 1024
FLO = 10
F = 96
BLK = 32
REACH = 8
NOFF = 2 * REACH + 1
SEG = 16

NZ = 4
NY = 4
NX = 4
NC = 2
FSHARE = F // NZ
FG = 8
GROUPS = FSHARE // FG
PIECE = 2 * FSHARE
CH = 256
ROWS = 128
HALF = 128

STAGES = ((1, 0, 256), (3, 0, 256), (2, 0, 256), (0, 0, 256))
NS = len(STAGES)
AHEAD = 2
LAG = 1

LINE = tuple((dx, dc) for dx in (1, 3, 0) for dc in (0, 1) if (dx, dc) != (0, 0))


def taper_table():
    t = np.arange(L, dtype=np.int64)
    k = FLO + np.arange(F, dtype=np.int64)
    phase = 2.0 * math.pi * ((k[:, None] * t[None, :]) % L) / L
    taper = (0.5 - 0.5 * np.cos(2.0 * math.pi * t / L)) / math.sqrt(3.0 * L / 8.0)
    both = np.stack([np.cos(phase) * taper, -np.sin(phase) * taper])
    both = both.reshape(2, NZ, GROUPS, FG, L).transpose(1, 2, 0, 3, 4)
    return both.reshape(2 * F, L).astype(np.float32).astype(jnp.bfloat16)


def chan_of(y, x, c):
    return (y * NX + x) * NC + c


def spectra_kernel(
    rec, keep, table_hbm, own, left, right,
    near, helped, partial, summed, spec, table, kown, kbuf,
    load, a_send, a_recv, a_local, p_send, p_recv,
    b_send, b_recv, b_local, c_send, c_recv, k_send, k_recv,
):
    z = lax.axis_index("tm")
    ch = lax.axis_index("chan")
    y = ch // (NX * NC)
    x = lax.rem(ch // NC, NX)
    c = lax.rem(ch, NC)
    nchan = NY * NX * NC
    after = lax.rem(ch + 1, nchan)
    before = lax.rem(ch + nchan - 1, nchan)

    def side(core):
        return 1 - 2 * core

    def along(steps):
        return lax.rem(x + NX + steps, NX)

    ahead, behind = along(side(c)), along(-side(c))

    load_table = pltpu.make_async_copy(table_hbm, table, load)
    load_table.start()

    barrier = pltpu.get_barrier_semaphore()
    signals = 0
    for dx, dc in LINE:
        peer = chan_of(y, lax.rem(x + dx, NX), lax.rem(c + dc, NC))
        pl.semaphore_signal(barrier, inc=1, device_id=(z, peer), device_id_type=MESH)
        signals += 1
    for dy in range(NY):
        for dz in range(NZ):
            if dy or dz:
                pl.semaphore_signal(
                    barrier, inc=1,
                    device_id=(lax.rem(z + dz, NZ), chan_of(lax.rem(y + dy, NY), x, c)),
                    device_id_type=MESH,
                )
                signals += 1
    for neighbour in (after, before):
        pl.semaphore_signal(barrier, inc=1, device_id=(z, neighbour), device_id_type=MESH)
        signals += 1

    pl.semaphore_wait(barrier, signals)

    def rows_of(group_x, group_c, j):
        dy, first, width = STAGES[j]
        column = chan_of(lax.rem(y + dy, NY), group_x, group_c) * CH + first
        return rec.at[:, pl.ds(pl.multiple_of(column, HALF), width)]

    def place(buffer, j, part):
        rows = pl.ds(pl.multiple_of(part * NC * ROWS + c * ROWS, ROWS), ROWS)
        return buffer.at[j, rows, pl.ds(0, STAGES[j][2])]

    def gather(j):
        to_helped, to_near = [], []
        n = 0
        for e in (0, 1):
            core = lax.rem(c + e, NC)
            s = side(core)
            for copies, buffer, part, group_x, target_x in (
                (to_helped, helped, 1, along(2), along(-s)),
                (to_near, near, 1, along(s), along(s)),
                (to_helped, helped, 0, along(-s), x),
                (to_near, near, 0, x, x),
            ):
                source, target = rows_of(group_x, core, j), place(buffer, j, part)
                if part == 0 and e == 0:
                    copy = pltpu.make_async_copy(
                        source, target, a_local.at[j, 0 if buffer is helped else 1]
                    )
                else:
                    copy = pltpu.make_async_remote_copy(
                        src_ref=source,
                        dst_ref=target,
                        send_sem=a_send.at[j, n],
                        recv_sem=a_recv.at[j, n],
                        device_id=(z, chan_of(y, target_x, core)),
                        device_id_type=MESH,
                    )
                    n += 1
                copy.start()
                copies.append((copy, part == 0 and e == 0))
        return to_helped, to_near

    gathers = [gather(j) for j in range(AHEAD)]
    lane_block = lax.broadcasted_iota(jnp.int32, (1, CH), 1) // BLK
    for s in range(NZ):
        spread = jnp.zeros((1, CH), jnp.int32)
        for b in range(CH // BLK):
            spread = jnp.where(lane_block == b, keep[s, b], spread)
        kown[s : s + 1, :] = spread.astype(jnp.float32)
    kown[NY:8, :] = jnp.zeros((8 - NY, CH), jnp.float32)
    keeps = []
    for n, ky in enumerate((1, 2, 3)):
        copy = pltpu.make_async_remote_copy(
            src_ref=kown,
            dst_ref=kbuf.at[y],
            send_sem=k_send.at[n],
            recv_sem=k_recv.at[n],
            device_id=(z, chan_of(lax.rem(y + ky, NY), x, c)),
            device_id_type=MESH,
        )
        copy.start()
        keeps.append(copy)

    def half_sum(buffer, j, chips):
        width = STAGES[j][2]
        total = jnp.zeros((2 * F, width), jnp.float32)
        energy = jnp.zeros((1, width), jnp.float32)
        for part, chip in enumerate(chips):
            data = buffer[j, part * NC * ROWS : (part + 1) * NC * ROWS, 0:width]
            columns = pl.ds(pl.multiple_of(chip * (NC * ROWS), NC * ROWS), NC * ROWS)
            total = total + jnp.dot(table[:, columns], data, preferred_element_type=jnp.float32)
            wide = data.astype(jnp.float32)
            energy = energy + jnp.sum(wide * wide, axis=0, keepdims=True)
        return total, energy

    def arrive(copies):
        for copy, local in copies:
            copy.wait() if local else copy.wait_recv()

    def pass_on(j):
        arrive(gathers[j][0])
        if len(gathers) < NS:
            gathers.append(gather(len(gathers)))
        total, energy = half_sum(helped, j, (x, ahead))
        width = STAGES[j][2]
        partial[j, 0 : 2 * F, 0:width] = total
        partial[j, 2 * F :, 0:width] = jnp.broadcast_to(energy, (8, width))
        copy = pltpu.make_async_remote_copy(
            src_ref=partial.at[j, :, pl.ds(0, width)],
            dst_ref=summed.at[j, :, pl.ds(0, width)],
            send_sem=p_send.at[j],
            recv_sem=p_recv.at[j],
            device_id=(z, chan_of(y, behind, c)),
            device_id_type=MESH,
        )
        copy.start()
        passed.append(copy)

    def halo(j):
        dy, first, width = STAGES[j]
        source = lax.rem(y + NY - dy, NY)
        copies = []
        for n, (neighbour, into) in enumerate(((after, left), (before, right))):
            copy = pltpu.make_async_remote_copy(
                src_ref=own.at[source, :, :, pl.ds(first, width)],
                dst_ref=into.at[source, :, :, pl.ds(first, width)],
                send_sem=c_send.at[j, n],
                recv_sem=c_recv.at[j, n],
                device_id=(z, neighbour),
                device_id_type=MESH,
            )
            copy.start()
            copies.append(copy)
        return copies

    def spread_arrived(j):
        for copy, local in spreads[j]:
            copy.wait() if local else copy.wait_recv()

    def finish(j):
        dy, first, width = STAGES[j]
        q = lax.rem(y + dy, NY)
        arrive(gathers[j][1])
        total, energy = half_sum(near, j, (x, behind))
        passed[j].wait_recv()
        energy = energy + summed[j, 2 * F : 2 * F + 1, 0:width]
        lanes = slice(first, first + width)
        kept = kown[pl.ds(y, 1), lanes] if dy == 0 else kbuf[q, pl.ds(y, 1), lanes]
        scale = lax.rsqrt(energy * (1.0 / L) + 1e-06) * kept
        raw = total + summed[j, 0 : 2 * F, 0:width]
        spec[j, :, :, 0:width] = (raw * scale).astype(jnp.bfloat16).reshape(NZ, PIECE, width)
        sent = []
        for dz in (2, 1, 3, 0):
            pz = lax.rem(z + dz, NZ)
            source = spec.at[j, pz, :, pl.ds(0, width)]
            target = own.at[y, z, :, pl.ds(first, width)]
            if dy == 0 and dz == 0:
                copy = pltpu.make_async_copy(source, target, b_local.at[j])
            else:
                copy = pltpu.make_async_remote_copy(
                    src_ref=source,
                    dst_ref=target,
                    send_sem=b_send.at[j, dz],
                    recv_sem=b_recv.at[j, dz],
                    device_id=(pz, chan_of(q, x, c)),
                    device_id_type=MESH,
                )
            copy.start()
            sent.append((copy, dy == 0 and dz == 0))
        spreads.append(sent)

    load_table.wait()
    passed, spreads, halos = [], [], []
    for j in range(NS):
        pass_on(j)
        for i in range(len(halos), j - 2):
            spread_arrived(i)
            halos.append(halo(i))
        if j == 0:
            for copy in keeps:
                copy.wait_recv()
        if j >= LAG:
            finish(j - LAG)
    for j in range(NS - LAG, NS):
        finish(j)
    for j in range(len(halos), NS):
        spread_arrived(j)
        halos.append(halo(j))

    for stage in gathers:
        for copies in stage:
            for copy, local in copies:
                if not local:
                    copy.wait_send()
    for copy in keeps + passed:
        copy.wait_send()
    for sent in spreads:
        for copy, local in sent:
            if not local:
                copy.wait_send()
    for pair in halos:
        for copy in pair:
            copy.wait()

    @pl.when(ch == 0)
    def _():
        left[...] = jnp.zeros_like(left)

    @pl.when(ch == nchan - 1)
    def _():
        right[...] = jnp.zeros_like(right)


def gather_spectra(records, keep, table):
    window = jax.ShapeDtypeStruct((NY, NZ, PIECE, CH), jnp.bfloat16)
    vmem = pl.BlockSpec(memory_space=pltpu.VMEM)
    hbm = pl.BlockSpec(memory_space=pl.ANY)
    dma = pltpu.SemaphoreType.DMA
    half = pltpu.VMEM((NS, 2 * NC * ROWS, CH), jnp.bfloat16)
    sums = pltpu.VMEM((NS, 2 * F + 8, CH), jnp.float32)
    return pl.pallas_call(
        spectra_kernel,
        out_shape=(window, window, window),
        in_specs=[hbm, pl.BlockSpec(memory_space=pltpu.SMEM), hbm],
        out_specs=(vmem, vmem, vmem),
        scratch_shapes=[
            half, half, sums, sums,
            pltpu.VMEM((NS, NZ, PIECE, CH), jnp.bfloat16),
            pltpu.VMEM((2 * F, L), jnp.bfloat16),
            pltpu.VMEM((8, CH), jnp.float32),
            pltpu.VMEM((NY, 8, CH), jnp.float32),
            dma, dma((NS, 6)), dma((NS, 6)), dma((NS, 2)), dma((NS,)), dma((NS,)),
            dma((NS, NZ)), dma((NS, NZ)), dma((NS,)),
            dma((NS, 2)), dma((NS, 2)), dma((NY - 1,)), dma((NY - 1,)),
        ],
        compiler_params=pltpu.CompilerParams(
            collective_id=0, has_side_effects=True, vmem_limit_bytes=211 << 18
        ),
        cost_estimate=pl.CostEstimate(
            flops=2 * 2 * F * L * NY * CH, bytes_accessed=2 * NY * L * CH, transcendentals=0
        ),
        name="gather_spectra",
    )(records, keep, table)


def cross_kernel(own, left, right, out, turned, weights, made, sem):
    terms = SEG * 2 * FG
    reach = NOFF * BLK + HALF - BLK
    lane_block = lax.broadcasted_iota(jnp.int32, (BLK, HALF), 1) // BLK
    row = lax.rem(lax.broadcasted_iota(jnp.int32, (terms, HALF), 0), FG)

    def prepare(g):
        for w, window in enumerate((left, own, right)):
            rows = window[:, :, g * 2 * FG : (g + 1) * 2 * FG, :].reshape(terms, CH)
            turned[g, w * CH : (w + 1) * CH, :] = rows.T
            if w == 1:
                wide = (rows.astype(jnp.float32) * (1.0 / SEG)).reshape(SEG, 2, FG, CH)
                plain = wide.reshape(terms, CH).astype(jnp.bfloat16)
                swapped = jnp.stack([wide[:, 1], -wide[:, 0]], 1)
                swapped = swapped.reshape(terms, CH).astype(jnp.bfloat16)
                for h in range(2):
                    weights[g, h, :, 0:HALF] = plain[:, h * HALF : (h + 1) * HALF]
                    weights[g, h, :, HALF : 2 * HALF] = swapped[:, h * HALF : (h + 1) * HALF]

    prepare(0)
    for g in range(GROUPS):
        for f8 in range(FG):
            if f8 == FG // 2 and g + 1 < GROUPS:
                prepare(g + 1)
            f = g * FG + f8
            chosen = jnp.where(row == f8, 1.0, 0.0).astype(jnp.bfloat16)
            chosen = jnp.concatenate([chosen, chosen], 1)
            for h in range(2):
                product = jnp.dot(
                    turned[g, h * HALF : h * HALF + reach, :],
                    weights[g, h] * chosen,
                    preferred_element_type=jnp.float32,
                )
                for part in range(2):
                    side = product[:, part * HALF : (part + 1) * HALF]
                    blocks = [side[r : r + BLK] for r in range(0, reach, BLK)]
                    for k in range(NOFF):
                        picked = blocks[k]
                        for i in range(1, HALF // BLK):
                            picked = jnp.where(lane_block == i, blocks[k + i], picked)
                        made[part, f, k, :, h * HALF : (h + 1) * HALF] = picked.astype(jnp.bfloat16)
            pltpu.make_async_copy(made.at[:, pl.ds(f, 1)], out.at[:, pl.ds(f, 1)], sem).start()
    pltpu.make_async_copy(made, out, sem).wait()


def cross_products(own, left, right):
    terms = SEG * 2 * FG
    vmem = pl.BlockSpec(memory_space=pltpu.VMEM)
    result = (2, FSHARE, NOFF, BLK, CH)
    return pl.pallas_call(
        cross_kernel,
        out_shape=jax.ShapeDtypeStruct(result, jnp.bfloat16),
        in_specs=[vmem, vmem, vmem],
        out_specs=pl.BlockSpec(memory_space=pl.ANY),
        scratch_shapes=[
            pltpu.VMEM((GROUPS, 3 * CH, terms), jnp.bfloat16),
            pltpu.VMEM((GROUPS, 2, terms, 2 * HALF), jnp.bfloat16),
            pltpu.VMEM(result, jnp.bfloat16),
            pltpu.SemaphoreType.DMA,
        ],
        compiler_params=pltpu.CompilerParams(vmem_limit_bytes=48 << 20),
        name="cross_products",
    )(own, left, right)


def shards(table, records, segment_keep):
    own, left, right = gather_spectra(records, segment_keep, table)
    return cross_products(own, left, right)


def solution(mesh):
    in_specs = (P(None, None), P(("tm", "chan"), None), P("tm", "chan"))
    out_specs = P(None, "tm", None, None, "chan")
    call = jax.shard_map(
        shards, mesh=mesh, in_specs=in_specs, out_specs=out_specs, check_vma=False
    )
    table = taper_table()

    def run(records, segment_keep):
        return call(jnp.asarray(table), records, segment_keep)

    return run
```
